32 devices in a mesh: dp: 8 (over z, x), own: 4 (over y, core).
Axes of the slice: x: 2, y: 2, z: 4, core: 2. Of those that a mesh axis runs over, the one named last changes fastest.
Arguments:
- grads: float32 [8, 4, 1024, 1024], P('dp', None, 'own'), may hold values from -0.27 to 0.27
- owner_map: int32 [4], replicated, may hold values from 0 to 7, as said below
- stat_left: float32 [8, 1024, 1024], P('own', 'dp'), as said below
- stat_right: float32 [8, 1024, 1024], P('own', 'dp'), as said below
- root_left: bfloat16 [8, 1024, 1024], P('own', 'dp'), as said below
- root_right: bfloat16 [8, 1024, 1024], P('own', 'dp'), as said below
- master: float32 [8, 1024, 1024], P('own', 'dp'), may hold values from -4 to 4
- moment_first: float32 [8, 1024, 1024], P('own', 'dp'), may hold values from -0.6 to 0.6
- moment_second: float32 [8, 1024, 1024], P('own', 'dp'), may hold values from 0.001 to 1, as said below
Outputs:
- left_next: float32 [8, 1024, 1024], P('own', 'dp')
- right_next: float32 [8, 1024, 1024], P('own', 'dp')
- master_next: float32 [8, 1024, 1024], P('own', 'dp')
- first_next: float32 [8, 1024, 1024], P('own', 'dp')
- second_next: float32 [8, 1024, 1024], P('own', 'dp')
- weights_out: bfloat16 [4, 1024, 1024], P(None, ('dp', 'own'))
The draws below stay inside these ranges and needn't reach their ends.
Inputs may be any that keep to these rules, and one draw needn't show every extreme that they name: `owner_map`: no two blocks share a slot. In every draw all 2 slots of some owner are taken, and so are slots 0 and 7. `root_left`: symmetric in its last two dimensions. `root_right`: symmetric in its last two dimensions. `stat_left`: symmetric in its last two dimensions. `stat_right`: symmetric in its last two dimensions. `moment_second`: Positive.
All inputs are finite; a program needn't handle non-finite values.
Results may differ from the reference program's by a relative error of at most 0.0045.
Values may be sent and summed in bfloat16 or wider, within the bound.
A program may use at most 128 MiB of HBM per device.

```python
import jax
import jax.numpy as jnp
from jax import lax

B = 1024
SLOTS = 2
BLOCKS = 4
OWNED = 8
GROUPS = 8


def symmetric_blocks(key, exponent):
    normals = jax.random.normal(jax.random.fold_in(key, 11), (OWNED, B, B), jnp.float32)
    symmetric = (normals + jnp.swapaxes(normals, 1, 2)) * 0.5 ** 0.5 / B ** 0.5
    diagonal = jax.random.uniform(jax.random.fold_in(key, 12), (OWNED, B), jnp.float32, 1.0, 2.0)
    identity = (jnp.arange(B)[:, None] == jnp.arange(B)[None, :]).astype(jnp.float32)
    matrix = symmetric + identity[None, :, :] * diagonal[:, :, None]
    position = jnp.arange(B, dtype=jnp.float32) / B
    row_scale = 10.0 ** (exponent * position)
    return matrix * row_scale[None, :, None] * row_scale[None, None, :]


def draw_owner_map(key, part):
    busiest = jax.random.randint(jax.random.fold_in(key, 21), (), 0, OWNED // SLOTS)
    priority = jax.random.permutation(jax.random.fold_in(key, 22), OWNED).astype(jnp.int32)
    indices = jnp.arange(OWNED, dtype=jnp.int32)
    forced = (indices == 0) | (indices == OWNED - 1) | (indices // SLOTS == busiest)
    scores = priority + OWNED * forced.astype(jnp.int32)
    ordering = jnp.argsort(-scores, stable=True).astype(jnp.int32)
    chosen = ordering[:BLOCKS]
    shuffle = jax.random.permutation(jax.random.fold_in(key, 23), BLOCKS)
    return chosen[shuffle].astype(jnp.int32)


def draw_stat_left(key, part):
    return symmetric_blocks(jax.random.fold_in(key, 31), 0.0)


def draw_stat_right(key, part):
    return symmetric_blocks(jax.random.fold_in(key, 32), 0.0)


def draw_root_left(key, part):
    return symmetric_blocks(jax.random.fold_in(key, 33), 1.0).astype(jnp.bfloat16)


def draw_root_right(key, part):
    return symmetric_blocks(jax.random.fold_in(key, 34), 0.5).astype(jnp.bfloat16)


def draw_moment_second(key, part):
    uniforms = jax.random.uniform(jax.random.fold_in(key, 35), (OWNED, B, B), jnp.float32)
    position = jnp.arange(B, dtype=jnp.float32) / B
    return 0.001 * 10.0 ** (uniforms + 2.0 * position[None, :, None])


def spiked(values, rng, source, target, blocks, factor):
    owner, partner = [(jnp.arange(values.shape[dim]) // (values.shape[dim] // blocks)).reshape([-1 if axis == dim else 1 for axis in range(values.ndim)]) for dim in (source, target)]
    chosen = jax.random.permutation(rng, blocks)[partner]
    strong = (owner == chosen) | (owner == (partner + blocks // 2) % blocks)
    return jnp.where(strong, factor * values, values)


def block_levels(own_key, dims, cuts, least, high):
    def one(dim, blocks):
        draws = jax.random.uniform(jax.random.fold_in(jax.random.fold_in(own_key, 6), dim), (blocks,), jnp.float32, least / len(cuts), high / len(cuts))
        return jnp.repeat(jnp.exp(draws), dims[dim] // blocks).reshape((-1,) + (1,) * (len(dims) - dim - 1))

    level = one(*cuts[0])
    for cut in cuts[1:]:
        level = level * one(*cut)
    return level


def bell_draw(own_key, dims, deviation, limit, cuts=(), kind=jnp.bfloat16):
    values = deviation * jax.random.normal(own_key, dims, jnp.float32)
    if cuts:
        values = values * block_levels(own_key, dims, cuts, -0.22, 0.18)
    return jnp.clip(values, -limit, limit).astype(kind)


def bell_draw_with(own_key, shape, scale, reach, shards, heavy, kind=jnp.bfloat16):
    array = scale * jax.random.normal(own_key, shape, jnp.float32)
    if shards:
        array = array * block_levels(own_key, shape, shards, -0.22, 0.18)
    return jnp.clip(spiked(array, jax.random.fold_in(own_key, 3), *heavy), -reach, reach).astype(kind)


def setup_inputs(seed: int = 0) -> dict:
    key_of = jax.random.split(jax.random.key(seed), 10)
    grads = bell_draw_with(key_of[0], (GROUPS, BLOCKS, B, B), 0.045, 0.27, ((0, 8), (2, 4)), (0, 2, 8, 2.0), jnp.float32)
    owner_map = draw_owner_map(jax.random.fold_in(key_of[9], 71), 0)
    stat_left = draw_stat_left(jax.random.fold_in(key_of[9], 71), 0)
    stat_right = draw_stat_right(jax.random.fold_in(key_of[9], 71), 0)
    root_left = draw_root_left(jax.random.fold_in(key_of[9], 71), 0)
    root_right = draw_root_right(jax.random.fold_in(key_of[9], 71), 0)
    master = bell_draw(key_of[6], (OWNED, B, B), 1.0, 4.0, ((0, 4), (1, 8)), jnp.float32)
    moment_first = bell_draw(key_of[7], (OWNED, B, B), 0.1, 0.6, ((0, 4), (1, 8)), jnp.float32)
    moment_second = draw_moment_second(jax.random.fold_in(key_of[9], 71), 0)
    return dict(grads=grads, owner_map=owner_map, stat_left=stat_left, stat_right=stat_right, root_left=root_left, root_right=root_right, master=master, moment_first=moment_first, moment_second=moment_second)


stat_decay = 0.9
first_decay = 0.9
second_decay = 0.99
learn_rate = 0.25

def refresh(block_items):
    gradient, left_stat, right_stat, root_left, root_right, weight, first_moment, second_moment = block_items
    highest = lax.Precision.HIGHEST
    left_next = stat_decay * left_stat + (1.0 - stat_decay) * jnp.dot(gradient, gradient.T, precision=highest, preferred_element_type=jnp.float32)
    right_next = stat_decay * right_stat + (1.0 - stat_decay) * jnp.dot(gradient.T, gradient, precision=highest, preferred_element_type=jnp.float32)
    first_next = first_decay * first_moment + (1.0 - first_decay) * gradient
    second_next = second_decay * second_moment + (1.0 - second_decay) * gradient * gradient
    adam_step = first_next / (jnp.sqrt(second_next) + 1e-08)
    product = jnp.dot(gradient.astype(jnp.bfloat16), root_right, preferred_element_type=jnp.float32).astype(jnp.bfloat16)
    direction = jnp.dot(root_left, product, preferred_element_type=jnp.float32)
    graft = jnp.sqrt(jnp.sum(adam_step * adam_step)) / (jnp.sqrt(jnp.sum(direction * direction)) + 1e-06)
    weight_next = weight - learn_rate * graft * direction
    return (left_next, right_next, weight_next, first_next, second_next)

def reference(grads, owner_map, stat_left, stat_right, root_left, root_right, master, moment_first, moment_second):
    summed = lax.optimization_barrier(jnp.sum(grads, axis=0))
    picked = tuple((jnp.take(states, owner_map, axis=0) for states in (stat_left, stat_right, root_left, root_right, master, moment_first, moment_second)))
    results = lax.map(refresh, (summed,) + picked)
    befores = (stat_left, stat_right, master, moment_first, moment_second)
    updated = tuple((before.at[owner_map].set(after) for before, after in zip(befores, results)))
    weights_out = results[2].astype(jnp.bfloat16)
    return (updated[0], updated[1], updated[2], updated[3], updated[4], weights_out)
```

```python
import functools

import jax
import jax.numpy as jnp
from jax import lax
from jax.experimental import pallas as pl
from jax.experimental.pallas import tpu as pltpu
from jax.sharding import PartitionSpec as P

stat_decay = 0.9
first_decay = 0.9
second_decay = 0.99
learn_rate = 0.25

VM = pltpu.VMEM
MIB = 1 << 20


def remote(src, dst, send, recv, dp, own):
    return pltpu.make_async_remote_copy(
        src_ref=src,
        dst_ref=dst,
        send_sem=send,
        recv_sem=recv,
        device_id=(dp, own),
        device_id_type=pl.DeviceIdType.MESH,
    )


def greet(dps, owns):
    dp, own = lax.axis_index("dp"), lax.axis_index("own")
    barrier = pltpu.get_barrier_semaphore()
    for k in range(1, dps):
        pl.semaphore_signal(barrier, inc=1, device_id=(lax.rem(dp + k, dps), own), device_id_type=pl.DeviceIdType.MESH)
    for k in range(1, owns):
        pl.semaphore_signal(barrier, inc=1, device_id=(dp, lax.rem(own + k, owns)), device_id_type=pl.DeviceIdType.MESH)
    pl.semaphore_wait(barrier, dps + owns - 2)


class Gather:
    def __init__(self, piece, nz, sems):
        self.piece, self.nz = piece, nz
        self.zs, self.zr, self.xs, self.xr = sems
        dp = lax.axis_index("dp")
        self.own = lax.axis_index("own")
        self.z, self.x = dp // 2, lax.rem(dp, 2)

    def along(self, way, t):
        sign = 1 - 2 * way
        at = self.z - sign * t
        there = self.z + sign
        ok = (at >= 0) & (at < self.nz) & (there >= 0) & (there < self.nz)
        ref = self.piece(at * 2 + self.x)
        return ok, remote(ref, ref, self.zs.at[way, t], self.zr.at[way, t], there * 2 + self.x, self.own)

    def across(self, way, t):
        sign = 1 - 2 * way
        at = self.z - sign * t
        ok = (at >= 0) & (at < self.nz)
        ref = self.piece(at * 2 + self.x)
        return ok, remote(ref, ref, self.xs.at[way, t], self.xr.at[way, t], self.z * 2 + 1 - self.x, self.own)

    def came(self, way, t):
        sign = 1 - 2 * way
        at = self.z - sign * (t + 1)
        ok = (at >= 0) & (at < self.nz)
        ref = self.piece(at * 2 + self.x)
        return ok, remote(ref, ref, self.zs.at[way, t], self.zr.at[way, t], self.z * 2 + 1 - self.x, self.own)

    def crossed(self, way, t):
        sign = 1 - 2 * way
        at = self.z - sign * t
        ok = (at >= 0) & (at < self.nz)
        ref = self.piece(at * 2 + 1 - self.x)
        return ok, remote(ref, ref, self.xs.at[way, t], self.xr.at[way, t], self.z * 2 + 1 - self.x, self.own)

    def start(self):
        for way in range(2):
            ok, copy = self.along(way, 0)
            pl.when(ok)(copy.start)
        self.across(0, 0)[1].start()

    def step(self, t):
        for way in range(2):
            ok, copy = self.came(way, t)
            pl.when(ok)(copy.wait_recv)
            if t + 1 < self.nz - 1:
                ok, copy = self.along(way, t + 1)
                pl.when(ok)(copy.start)
            ok, copy = self.across(way, t + 1)
            pl.when(ok)(copy.start)

    def finish(self):
        for t in range(self.nz):
            for way in range(1 if t == 0 else 2):
                ok, copy = self.crossed(way, t)
                pl.when(ok)(copy.wait_recv)
                ok, copy = self.across(way, t)
                pl.when(ok)(copy.wait_send)
        for t in range(self.nz - 1):
            for way in range(2):
                ok, copy = self.along(way, t)
                pl.when(ok)(copy.wait_send)


def exchange_kernel(
    dps, owns, blocks, slots, part,
    pick, grad, root, whole, roots,
    landed, packed, p_send, p_recv, o_send, o_recv,
    gzs, gzr, gxs, gxr, rzs, rzr, rxs, rxr, own_sem,
):
    dp, own = lax.axis_index("dp"), lax.axis_index("own")
    nz = dps // 2
    mine = pltpu.make_async_copy(root, roots.at[:, dp], own_sem)
    mine.start()
    greet(dps, owns)

    def scatter(k):
        there = lax.rem(dp + k, dps)
        rows = pl.ds(pl.multiple_of(there * part, part), part)
        return remote(grad.at[:, rows, :], landed.at[k - 1], p_send.at[k - 1], p_recv.at[k - 1], there, own)

    for k in range(1, dps):
        scatter(k).start()
    mine.wait()
    fetch = Gather(lambda at: roots.at[:, at], nz, (rzs, rzr, rxs, rxr))
    fetch.start()
    for t in range(nz - 2):
        fetch.step(t)
    for k in range(1, dps):
        scatter(k).wait_recv()
    rows = pl.ds(pl.multiple_of(dp * part, part), part)
    for b in range(blocks):
        total = grad[b, rows, :].astype(jnp.float32)
        for k in range(1, dps):
            total = total + landed[k - 1, b].astype(jnp.float32)
        packed[owns * slots + b] = total.astype(jnp.bfloat16)
    for s in range(owns * slots):
        total = pick[s] * packed[owns * slots].astype(jnp.float32)
        for b in range(1, blocks):
            total = total + pick[b * owns * slots + s] * packed[owns * slots + b].astype(jnp.float32)
        packed[s] = total.astype(jnp.bfloat16)

    def deliver(k):
        there = lax.rem(own + k, owns)
        return remote(
            packed.at[pl.ds(there * slots, slots)], whole.at[:, own, dp], o_send.at[k - 1], o_recv.at[k - 1], dp, there
        )

    def delivered(k):
        source = lax.rem(own + owns - k, owns)
        return remote(
            packed.at[pl.ds(own * slots, slots)], whole.at[:, source, dp], o_send.at[k - 1], o_recv.at[k - 1], dp, lax.rem(own + k, owns)
        )

    for k in range(1, owns):
        deliver(k).start()
    for s in range(slots):
        whole[s, own, dp] = packed[own * slots + s]
    fetch.step(nz - 2)
    for k in range(1, owns):
        delivered(k).wait_recv()
    spread = Gather(lambda at: whole.at[:, :, at], nz, (gzs, gzr, gxs, gxr))
    spread.start()
    for t in range(nz - 1):
        spread.step(t)
    fetch.finish()
    spread.finish()
    for k in range(1, owns):
        deliver(k).wait_send()
    for k in range(1, dps):
        scatter(k).wait_send()


def exchange(pick, grad, root, dps, owns):
    blocks, rows, cols = grad.shape
    slots, rows_dev = root.shape[:2]
    part = rows // dps
    nz = dps // 2
    dma = pltpu.SemaphoreType.DMA
    return pl.pallas_call(
        functools.partial(exchange_kernel, dps, owns, blocks, slots, part),
        out_shape=(
            jax.ShapeDtypeStruct((slots, owns, dps, part, cols), jnp.bfloat16),
            jax.ShapeDtypeStruct((slots, dps, rows_dev, cols), jnp.bfloat16),
        ),
        in_specs=[pl.BlockSpec(memory_space=pltpu.SMEM)] + [pl.BlockSpec(memory_space=VM)] * 2,
        out_specs=(pl.BlockSpec(memory_space=VM),) * 2,
        scratch_shapes=[
            VM((dps - 1, blocks, part, cols), jnp.bfloat16),
            VM((owns * slots + blocks, part, cols), jnp.bfloat16),
            dma((dps - 1,)),
            dma((dps - 1,)),
            dma((owns - 1,)),
            dma((owns - 1,)),
        ]
        + [dma((2, nz))] * 8
        + [dma],
        compiler_params=pltpu.CompilerParams(collective_id=0, has_side_effects=True, vmem_limit_bytes=40 * MIB),
    )(pick, grad, root)


def finish_kernel(dps, owns, slots, part, squares, direction, master, sums, out, held, shares, s_send, s_recv, w_send, w_recv):
    dp, own = lax.axis_index("dp"), lax.axis_index("own")
    greet(dps, owns)

    def tell(k):
        return remote(squares, held.at[k - 1], s_send.at[k - 1], s_recv.at[k - 1], lax.rem(dp + k, dps), own)

    for k in range(1, dps):
        tell(k).start()
    for k in range(1, dps):
        tell(k).wait_recv()
    total = squares[...]
    for k in range(1, dps):
        total = total + held[k - 1]
    sums[...] = total
    for s in range(slots):
        graft = jnp.sqrt(total[s : s + 1, :1]) / (jnp.sqrt(total[slots + s : slots + s + 1, :1]) + 1e-06)
        for o in range(owns):
            rows = pl.ds(o * part, part)
            shares[o, s] = (master[s, rows, :] - learn_rate * graft * direction[s, rows, :]).astype(jnp.bfloat16)

    def deliver(k):
        there = lax.rem(own + k, owns)
        return remote(shares.at[there], out.at[own], w_send.at[k - 1], w_recv.at[k - 1], dp, there)

    def delivered(k):
        source = lax.rem(own + owns - k, owns)
        return remote(shares.at[own], out.at[source], w_send.at[k - 1], w_recv.at[k - 1], dp, lax.rem(own + k, owns))

    for k in range(1, owns):
        deliver(k).start()
    out[own] = shares[own]
    for k in range(1, owns):
        delivered(k).wait_recv()
    for k in range(1, owns):
        deliver(k).wait_send()
    for k in range(1, dps):
        tell(k).wait_send()


def finish(squares, direction, master, dps, owns):
    slots, rows_dev, cols = master.shape
    part = rows_dev // owns
    dma = pltpu.SemaphoreType.DMA
    return pl.pallas_call(
        functools.partial(finish_kernel, dps, owns, slots, part),
        out_shape=(
            jax.ShapeDtypeStruct(squares.shape, jnp.float32),
            jax.ShapeDtypeStruct((owns, slots, part, cols), jnp.bfloat16),
        ),
        in_specs=[pl.BlockSpec(memory_space=VM)] * 3,
        out_specs=(pl.BlockSpec(memory_space=VM),) * 2,
        scratch_shapes=[
            VM((dps - 1,) + squares.shape, jnp.float32),
            VM((owns, slots, part, cols), jnp.bfloat16),
            dma((dps - 1,)),
            dma((dps - 1,)),
            dma((owns - 1,)),
            dma((owns - 1,)),
        ],
        compiler_params=pltpu.CompilerParams(collective_id=1, has_side_effects=True, vmem_limit_bytes=24 * MIB),
    )(squares, direction, master)


def whole_by_collectives(grads, owner_map, root_right, occupied, block_of):
    owners = lax.axis_size("own")
    slot_count, _, order_size = root_right.shape
    summed = lax.psum(grads[0], "dp")
    packed = jnp.stack(
        [lax.dynamic_index_in_dim(summed, block_of[s], 0, keepdims=False) for s in range(owners * slot_count)]
    )
    packed = jnp.where(occupied[:, None, None], packed, 0.0)
    packed = packed.reshape(owners, slot_count, summed.shape[1], order_size).astype(jnp.bfloat16)
    arrived = lax.all_to_all(packed, "own", split_axis=0, concat_axis=2, tiled=True)
    return (
        arrived.reshape(slot_count, order_size, order_size),
        lax.all_gather(root_right, "dp", axis=1, tiled=True),
    )


def per_device(
    grads,
    owner_map,
    stat_left,
    stat_right,
    root_left,
    root_right,
    master,
    moment_first,
    moment_second,
):
    owners, groups = lax.axis_size("own"), lax.axis_size("dp")
    slot_count, rows_dev, order_size = stat_left.shape
    blocks = owner_map.shape[0]
    owned_slots = owners * slot_count
    matches = owner_map[:, None] == jnp.arange(owned_slots, dtype=jnp.int32)[None, :]
    occupied = jnp.any(matches, axis=0)
    kernels = groups % 2 == 0 and (grads.shape[2] // groups) % 16 == 0 and (rows_dev // owners) % 16 == 0
    if kernels:
        pick = matches.astype(jnp.float32).reshape(-1)
        whole, right = exchange(pick, grads[0].astype(jnp.bfloat16), root_right, groups, owners)
        whole = whole.reshape(slot_count, order_size, order_size)
        right = right.reshape(slot_count, order_size, order_size)
    else:
        block_of = jnp.sum(jnp.where(matches, jnp.arange(blocks, dtype=jnp.int32)[:, None], 0), axis=0)
        whole, right = whole_by_collectives(grads, owner_map, root_right, occupied, block_of)
    first_row = lax.axis_index("dp") * rows_dev
    own_rows = lax.dynamic_slice_in_dim(whole, first_row, rows_dev, 1)
    own_cols = lax.dynamic_slice_in_dim(whole, first_row, rows_dev, 2)
    mixed = jnp.einsum("srk,skn->srn", root_left, whole, preferred_element_type=jnp.float32)
    direction = jnp.einsum(
        "srk,skn->srn", mixed.astype(jnp.bfloat16), right, preferred_element_type=jnp.float32
    )
    rows32 = own_rows.astype(jnp.float32)
    first_new = first_decay * moment_first + (1.0 - first_decay) * rows32
    second_new = second_decay * moment_second + (1.0 - second_decay) * rows32 * rows32
    adam_step = first_new / (jnp.sqrt(second_new) + 1e-08)
    square_sums = jnp.concatenate(
        [jnp.sum(adam_step * adam_step, axis=(1, 2)), jnp.sum(direction * direction, axis=(1, 2))]
    )
    if kernels:
        padded = jnp.pad(square_sums, (0, -2 * slot_count % 8))
        totals, delivered = finish(
            jnp.broadcast_to(padded[:, None], (padded.shape[0], 128)), direction, master, groups, owners
        )
        square_sums = totals[: 2 * slot_count, 0]
    else:
        square_sums = lax.psum(square_sums, "dp")
    graft = jnp.sqrt(square_sums[:slot_count]) / (jnp.sqrt(square_sums[slot_count:]) + 1e-06)
    master_new = master - learn_rate * graft[:, None, None] * direction
    if not kernels:
        shares = master_new.astype(jnp.bfloat16).reshape(slot_count, owners, rows_dev // owners, order_size)
        delivered = lax.all_to_all(shares, "own", split_axis=1, concat_axis=0, tiled=True)
    delivered = delivered.reshape(owned_slots, rows_dev // owners, order_size)
    left_new = stat_decay * stat_left + (1.0 - stat_decay) * jnp.einsum(
        "srk,snk->srn", own_rows, whole, preferred_element_type=jnp.float32
    )
    right_new = stat_decay * stat_right + (1.0 - stat_decay) * jnp.einsum(
        "skr,skn->srn", own_cols, whole, preferred_element_type=jnp.float32
    )
    occupied_mine = lax.dynamic_slice_in_dim(
        occupied, lax.axis_index("own") * slot_count, slot_count
    )[:, None, None]
    left_next = jnp.where(occupied_mine, left_new, stat_left)
    right_next = jnp.where(occupied_mine, right_new, stat_right)
    master_next = jnp.where(occupied_mine, master_new, master)
    first_next = jnp.where(occupied_mine, first_new, moment_first)
    second_next = jnp.where(occupied_mine, second_new, moment_second)
    weights_out = jnp.stack(
        [lax.dynamic_index_in_dim(delivered, owner_map[b], 0, keepdims=False) for b in range(blocks)]
    )
    return (left_next, right_next, master_next, first_next, second_next, weights_out)


def solution(mesh):
    state = P("own", "dp", None)
    return jax.shard_map(
        per_device,
        mesh=mesh,
        in_specs=(P("dp", None, "own", None), P()) + (state,) * 7,
        out_specs=(state,) * 5 + (P(None, ("dp", "own"), None),),
        check_vma=False,
    )
```

```python
import functools

import jax
import jax.numpy as jnp
from jax import lax
from jax.experimental import pallas as pl
from jax.experimental.pallas import tpu as pltpu
from jax.sharding import PartitionSpec as P

stat_decay = 0.9
first_decay = 0.9
second_decay = 0.99
learn_rate = 0.25

VM = pltpu.VMEM
MIB = 1 << 20


def remote(src, dst, send, recv, dp, own):
    return pltpu.make_async_remote_copy(
        src_ref=src,
        dst_ref=dst,
        send_sem=send,
        recv_sem=recv,
        device_id=(dp, own),
        device_id_type=pl.DeviceIdType.MESH,
    )


def greet(dps, owns):
    dp, own = lax.axis_index("dp"), lax.axis_index("own")
    barrier = pltpu.get_barrier_semaphore()
    for k in range(1, dps):
        pl.semaphore_signal(barrier, inc=1, device_id=(lax.rem(dp + k, dps), own), device_id_type=pl.DeviceIdType.MESH)
    for k in range(1, owns):
        pl.semaphore_signal(barrier, inc=1, device_id=(dp, lax.rem(own + k, owns)), device_id_type=pl.DeviceIdType.MESH)
    pl.semaphore_wait(barrier, dps + owns - 2)


class Gather:
    def __init__(self, piece, nz, sems):
        self.piece, self.nz = piece, nz
        self.zs, self.zr, self.xs, self.xr = sems
        dp = lax.axis_index("dp")
        self.own = lax.axis_index("own")
        self.z, self.x = dp // 2, lax.rem(dp, 2)

    def along(self, way, t):
        sign = 1 - 2 * way
        at = self.z - sign * t
        there = self.z + sign
        ok = (at >= 0) & (at < self.nz) & (there >= 0) & (there < self.nz)
        ref = self.piece(at * 2 + self.x)
        return ok, remote(ref, ref, self.zs.at[way, t], self.zr.at[way, t], there * 2 + self.x, self.own)

    def across(self, way, t):
        sign = 1 - 2 * way
        at = self.z - sign * t
        ok = (at >= 0) & (at < self.nz)
        ref = self.piece(at * 2 + self.x)
        return ok, remote(ref, ref, self.xs.at[way, t], self.xr.at[way, t], self.z * 2 + 1 - self.x, self.own)

    def came(self, way, t):
        sign = 1 - 2 * way
        at = self.z - sign * (t + 1)
        ok = (at >= 0) & (at < self.nz)
        ref = self.piece(at * 2 + self.x)
        return ok, remote(ref, ref, self.zs.at[way, t], self.zr.at[way, t], self.z * 2 + 1 - self.x, self.own)

    def crossed(self, way, t):
        sign = 1 - 2 * way
        at = self.z - sign * t
        ok = (at >= 0) & (at < self.nz)
        ref = self.piece(at * 2 + 1 - self.x)
        return ok, remote(ref, ref, self.xs.at[way, t], self.xr.at[way, t], self.z * 2 + 1 - self.x, self.own)

    def start(self):
        for way in range(2):
            ok, copy = self.along(way, 0)
            pl.when(ok)(copy.start)
        self.across(0, 0)[1].start()

    def step(self, t):
        for way in range(2):
            ok, copy = self.came(way, t)
            pl.when(ok)(copy.wait_recv)
            if t + 1 < self.nz - 1:
                ok, copy = self.along(way, t + 1)
                pl.when(ok)(copy.start)
            ok, copy = self.across(way, t + 1)
            pl.when(ok)(copy.start)

    def finish(self):
        for t in range(self.nz):
            for way in range(1 if t == 0 else 2):
                ok, copy = self.crossed(way, t)
                pl.when(ok)(copy.wait_recv)
                ok, copy = self.across(way, t)
                pl.when(ok)(copy.wait_send)
        for t in range(self.nz - 1):
            for way in range(2):
                ok, copy = self.along(way, t)
                pl.when(ok)(copy.wait_send)


def exchange_kernel(
    dps, owns, blocks, slots, part,
    pick, grad, root, whole, roots,
    halves, sums, landed, packed, x_send, x_recv, p_send, p_recv, o_send, o_recv,
    gzs, gzr, gxs, gxr, rzs, rzr, rxs, rxr, own_sem,
):
    dp, own = lax.axis_index("dp"), lax.axis_index("own")
    nz = dps // 2
    mine = pltpu.make_async_copy(root, roots.at[:, dp], own_sem)
    mine.start()
    greet(dps, owns)

    z, x = dp // 2, lax.rem(dp, 2)

    def chunk(at):
        return pl.ds(pl.multiple_of(at * part, part), part)

    def pair(k):
        there = lax.rem(z + k, nz)
        rows = chunk(there * 2 + 1 - x)
        return remote(grad.at[:, rows, :], halves.at[k], x_send.at[k], x_recv.at[k], z * 2 + 1 - x, own)

    def scatter(k):
        there = lax.rem(z + k, nz) * 2 + x
        return remote(sums.at[k - 1], landed.at[k - 1], p_send.at[k - 1], p_recv.at[k - 1], there, own)

    order = [nz // 2] + [k for k in range(1, nz) if k != nz // 2] + [0]
    for k in order:
        pair(k).start()
    mine.wait()
    fetch = Gather(lambda at: roots.at[:, at], nz, (rzs, rzr, rxs, rxr))
    fetch.start()
    for k in order[:-1]:
        pair(k).wait_recv()
        rows = chunk(lax.rem(z + k, nz) * 2 + x)
        for b in range(blocks):
            total = grad[b, rows, :].astype(jnp.float32) + halves[k, b].astype(jnp.float32)
            sums[k - 1, b] = total.astype(jnp.bfloat16)
        scatter(k).start()
    for t in range(nz - 2):
        fetch.step(t)
    pair(0).wait_recv()
    for k in range(1, nz):
        scatter(k).wait_recv()
    rows = chunk(dp)
    for b in range(blocks):
        total = grad[b, rows, :].astype(jnp.float32) + halves[0, b].astype(jnp.float32)
        for k in range(1, nz):
            total = total + landed[k - 1, b].astype(jnp.float32)
        packed[owns * slots + b] = total.astype(jnp.bfloat16)
    for s in range(owns * slots):
        total = pick[s] * packed[owns * slots].astype(jnp.float32)
        for b in range(1, blocks):
            total = total + pick[b * owns * slots + s] * packed[owns * slots + b].astype(jnp.float32)
        packed[s] = total.astype(jnp.bfloat16)

    def deliver(k):
        there = lax.rem(own + k, owns)
        return remote(
            packed.at[pl.ds(there * slots, slots)], whole.at[:, own, dp], o_send.at[k - 1], o_recv.at[k - 1], dp, there
        )

    def delivered(k):
        source = lax.rem(own + owns - k, owns)
        return remote(
            packed.at[pl.ds(own * slots, slots)], whole.at[:, source, dp], o_send.at[k - 1], o_recv.at[k - 1], dp, lax.rem(own + k, owns)
        )

    for k in range(1, owns):
        deliver(k).start()
    for s in range(slots):
        whole[s, own, dp] = packed[own * slots + s]
    fetch.step(nz - 2)
    for k in range(1, owns):
        delivered(k).wait_recv()
    spread = Gather(lambda at: whole.at[:, :, at], nz, (gzs, gzr, gxs, gxr))
    spread.start()
    for t in range(nz - 1):
        spread.step(t)
    fetch.finish()
    spread.finish()
    for k in range(1, owns):
        deliver(k).wait_send()
    for k in range(1, nz):
        scatter(k).wait_send()
    for k in range(nz):
        pair(k).wait_send()


def exchange(pick, grad, root, dps, owns):
    blocks, rows, cols = grad.shape
    slots, rows_dev = root.shape[:2]
    part = rows // dps
    nz = dps // 2
    dma = pltpu.SemaphoreType.DMA
    return pl.pallas_call(
        functools.partial(exchange_kernel, dps, owns, blocks, slots, part),
        out_shape=(
            jax.ShapeDtypeStruct((slots, owns, dps, part, cols), jnp.bfloat16),
            jax.ShapeDtypeStruct((slots, dps, rows_dev, cols), jnp.bfloat16),
        ),
        in_specs=[pl.BlockSpec(memory_space=pltpu.SMEM)] + [pl.BlockSpec(memory_space=VM)] * 2,
        out_specs=(pl.BlockSpec(memory_space=VM),) * 2,
        scratch_shapes=[
            VM((nz, blocks, part, cols), jnp.bfloat16),
            VM((nz - 1, blocks, part, cols), jnp.bfloat16),
            VM((nz - 1, blocks, part, cols), jnp.bfloat16),
            VM((owns * slots + blocks, part, cols), jnp.bfloat16),
            dma((nz,)),
            dma((nz,)),
            dma((nz - 1,)),
            dma((nz - 1,)),
            dma((owns - 1,)),
            dma((owns - 1,)),
        ]
        + [dma((2, nz))] * 8
        + [dma],
        compiler_params=pltpu.CompilerParams(collective_id=0, has_side_effects=True, vmem_limit_bytes=40 * MIB),
    )(pick, grad, root)


def finish_kernel(dps, owns, slots, part, squares, direction, master, sums, out, held, shares, s_send, s_recv, w_send, w_recv):
    dp, own = lax.axis_index("dp"), lax.axis_index("own")
    greet(dps, owns)

    def tell(k):
        return remote(squares, held.at[k - 1], s_send.at[k - 1], s_recv.at[k - 1], lax.rem(dp + k, dps), own)

    for k in range(1, dps):
        tell(k).start()
    for k in range(1, dps):
        tell(k).wait_recv()
    total = squares[...]
    for k in range(1, dps):
        total = total + held[k - 1]
    sums[...] = total
    for s in range(slots):
        graft = jnp.sqrt(total[s : s + 1, :1]) / (jnp.sqrt(total[slots + s : slots + s + 1, :1]) + 1e-06)
        for o in range(owns):
            rows = pl.ds(o * part, part)
            shares[o, s] = (master[s, rows, :] - learn_rate * graft * direction[s, rows, :]).astype(jnp.bfloat16)

    def deliver(k):
        there = lax.rem(own + k, owns)
        return remote(shares.at[there], out.at[own], w_send.at[k - 1], w_recv.at[k - 1], dp, there)

    def delivered(k):
        source = lax.rem(own + owns - k, owns)
        return remote(shares.at[own], out.at[source], w_send.at[k - 1], w_recv.at[k - 1], dp, lax.rem(own + k, owns))

    for k in range(1, owns):
        deliver(k).start()
    out[own] = shares[own]
    for k in range(1, owns):
        delivered(k).wait_recv()
    for k in range(1, owns):
        deliver(k).wait_send()
    for k in range(1, dps):
        tell(k).wait_send()


def finish(squares, direction, master, dps, owns):
    slots, rows_dev, cols = master.shape
    part = rows_dev // owns
    dma = pltpu.SemaphoreType.DMA
    return pl.pallas_call(
        functools.partial(finish_kernel, dps, owns, slots, part),
        out_shape=(
            jax.ShapeDtypeStruct(squares.shape, jnp.float32),
            jax.ShapeDtypeStruct((owns, slots, part, cols), jnp.bfloat16),
        ),
        in_specs=[pl.BlockSpec(memory_space=VM)] * 3,
        out_specs=(pl.BlockSpec(memory_space=VM),) * 2,
        scratch_shapes=[
            VM((dps - 1,) + squares.shape, jnp.float32),
            VM((owns, slots, part, cols), jnp.bfloat16),
            dma((dps - 1,)),
            dma((dps - 1,)),
            dma((owns - 1,)),
            dma((owns - 1,)),
        ],
        compiler_params=pltpu.CompilerParams(collective_id=1, has_side_effects=True, vmem_limit_bytes=24 * MIB),
    )(squares, direction, master)


def whole_by_collectives(grads, owner_map, root_right, occupied, block_of):
    owners = lax.axis_size("own")
    slot_count, _, order_size = root_right.shape
    summed = lax.psum(grads[0], "dp")
    packed = jnp.stack(
        [lax.dynamic_index_in_dim(summed, block_of[s], 0, keepdims=False) for s in range(owners * slot_count)]
    )
    packed = jnp.where(occupied[:, None, None], packed, 0.0)
    packed = packed.reshape(owners, slot_count, summed.shape[1], order_size).astype(jnp.bfloat16)
    arrived = lax.all_to_all(packed, "own", split_axis=0, concat_axis=2, tiled=True)
    return (
        arrived.reshape(slot_count, order_size, order_size),
        lax.all_gather(root_right, "dp", axis=1, tiled=True),
    )


def per_device(
    grads,
    owner_map,
    stat_left,
    stat_right,
    root_left,
    root_right,
    master,
    moment_first,
    moment_second,
):
    owners, groups = lax.axis_size("own"), lax.axis_size("dp")
    slot_count, rows_dev, order_size = stat_left.shape
    blocks = owner_map.shape[0]
    owned_slots = owners * slot_count
    matches = owner_map[:, None] == jnp.arange(owned_slots, dtype=jnp.int32)[None, :]
    occupied = jnp.any(matches, axis=0)
    kernels = groups % 2 == 0 and (grads.shape[2] // groups) % 16 == 0 and (rows_dev // owners) % 16 == 0
    if kernels:
        pick = matches.astype(jnp.float32).reshape(-1)
        whole, right = exchange(pick, grads[0].astype(jnp.bfloat16), root_right, groups, owners)
        whole = whole.reshape(slot_count, order_size, order_size)
        right = right.reshape(slot_count, order_size, order_size)
    else:
        block_of = jnp.sum(jnp.where(matches, jnp.arange(blocks, dtype=jnp.int32)[:, None], 0), axis=0)
        whole, right = whole_by_collectives(grads, owner_map, root_right, occupied, block_of)
    first_row = lax.axis_index("dp") * rows_dev
    own_rows = lax.dynamic_slice_in_dim(whole, first_row, rows_dev, 1)
    own_cols = lax.dynamic_slice_in_dim(whole, first_row, rows_dev, 2)
    mixed = jnp.einsum("srk,skn->srn", root_left, whole, preferred_element_type=jnp.float32)
    direction = jnp.einsum(
        "srk,skn->srn", mixed.astype(jnp.bfloat16), right, preferred_element_type=jnp.float32
    )
    rows32 = own_rows.astype(jnp.float32)
    first_new = first_decay * moment_first + (1.0 - first_decay) * rows32
    second_new = second_decay * moment_second + (1.0 - second_decay) * rows32 * rows32
    adam_step = first_new / (jnp.sqrt(second_new) + 1e-08)
    square_sums = jnp.concatenate(
        [jnp.sum(adam_step * adam_step, axis=(1, 2)), jnp.sum(direction * direction, axis=(1, 2))]
    )
    if kernels:
        padded = jnp.pad(square_sums, (0, -2 * slot_count % 8))
        totals, delivered = finish(
            jnp.broadcast_to(padded[:, None], (padded.shape[0], 128)), direction, master, groups, owners
        )
        square_sums = totals[: 2 * slot_count, 0]
    else:
        square_sums = lax.psum(square_sums, "dp")
    graft = jnp.sqrt(square_sums[:slot_count]) / (jnp.sqrt(square_sums[slot_count:]) + 1e-06)
    master_new = master - learn_rate * graft[:, None, None] * direction
    if not kernels:
        shares = master_new.astype(jnp.bfloat16).reshape(slot_count, owners, rows_dev // owners, order_size)
        delivered = lax.all_to_all(shares, "own", split_axis=1, concat_axis=0, tiled=True)
    delivered = delivered.reshape(owned_slots, rows_dev // owners, order_size)
    left_new = stat_decay * stat_left + (1.0 - stat_decay) * jnp.einsum(
        "srk,snk->srn", own_rows, whole, preferred_element_type=jnp.float32
    )
    right_new = stat_decay * stat_right + (1.0 - stat_decay) * jnp.einsum(
        "skr,skn->srn", own_cols, whole, preferred_element_type=jnp.float32
    )
    occupied_mine = lax.dynamic_slice_in_dim(
        occupied, lax.axis_index("own") * slot_count, slot_count
    )[:, None, None]
    left_next = jnp.where(occupied_mine, left_new, stat_left)
    right_next = jnp.where(occupied_mine, right_new, stat_right)
    master_next = jnp.where(occupied_mine, master_new, master)
    first_next = jnp.where(occupied_mine, first_new, moment_first)
    second_next = jnp.where(occupied_mine, second_new, moment_second)
    weights_out = jnp.stack(
        [lax.dynamic_index_in_dim(delivered, owner_map[b], 0, keepdims=False) for b in range(blocks)]
    )
    return (left_next, right_next, master_next, first_next, second_next, weights_out)


def solution(mesh):
    state = P("own", "dp", None)
    return jax.shard_map(
        per_device,
        mesh=mesh,
        in_specs=(P("dp", None, "own", None), P()) + (state,) * 7,
        out_specs=(state,) * 5 + (P(None, ("dp", "own"), None),),
        check_vma=False,
    )
```

```python
import functools

import jax
import jax.numpy as jnp
from jax import lax
from jax.experimental import pallas as pl
from jax.experimental.pallas import tpu as pltpu
from jax.sharding import PartitionSpec as P

stat_decay = 0.9
first_decay = 0.9
second_decay = 0.99
learn_rate = 0.25

VM = pltpu.VMEM
MIB = 1 << 20


def remote(src, dst, send, recv, dp, own):
    return pltpu.make_async_remote_copy(
        src_ref=src,
        dst_ref=dst,
        send_sem=send,
        recv_sem=recv,
        device_id=(dp, own),
        device_id_type=pl.DeviceIdType.MESH,
    )


def greet(dps, owns):
    dp, own = lax.axis_index("dp"), lax.axis_index("own")
    barrier = pltpu.get_barrier_semaphore()
    for k in range(1, dps):
        pl.semaphore_signal(barrier, inc=1, device_id=(lax.rem(dp + k, dps), own), device_id_type=pl.DeviceIdType.MESH)
    for k in range(1, owns):
        pl.semaphore_signal(barrier, inc=1, device_id=(dp, lax.rem(own + k, owns)), device_id_type=pl.DeviceIdType.MESH)
    pl.semaphore_wait(barrier, dps + owns - 2)


class Gather:
    def __init__(self, piece, main, side, nz, sems):
        self.piece, self.main, self.side, self.nz = piece, main, side, nz
        self.zs, self.zr, self.xs, self.xr, self.ss, self.sr = sems
        dp = lax.axis_index("dp")
        self.own = lax.axis_index("own")
        self.z, self.x = dp // 2, lax.rem(dp, 2)

    def along(self, way, t):
        sign = 1 - 2 * way
        at = self.z - sign * t
        there = self.z + sign
        ok = (at >= 0) & (at < self.nz) & (there >= 0) & (there < self.nz)
        ref = self.piece(at * 2 + self.x)
        return ok, remote(ref, ref, self.zs.at[way, t], self.zr.at[way, t], there * 2 + self.x, self.own)

    def across(self, way, t):
        sign = 1 - 2 * way
        at = self.z - sign * t
        ok = (at >= 0) & (at < self.nz)
        ref = (self.main if t else self.piece)(at * 2 + self.x)
        return ok, remote(ref, ref, self.xs.at[way, t], self.xr.at[way, t], self.z * 2 + 1 - self.x, self.own)

    def came(self, way, t):
        sign = 1 - 2 * way
        at = self.z - sign * (t + 1)
        ok = (at >= 0) & (at < self.nz)
        ref = self.piece(at * 2 + self.x)
        return ok, remote(ref, ref, self.zs.at[way, t], self.zr.at[way, t], self.z * 2 + 1 - self.x, self.own)

    def crossed(self, way, t):
        sign = 1 - 2 * way
        at = self.z - sign * t
        ok = (at >= 0) & (at < self.nz)
        ref = (self.main if t else self.piece)(at * 2 + 1 - self.x)
        return ok, remote(ref, ref, self.xs.at[way, t], self.xr.at[way, t], self.z * 2 + 1 - self.x, self.own)

    def aside(self, way, t):
        sign = 1 - 2 * way
        at = self.z - sign * t
        there = self.z + sign
        ok = (at >= 0) & (at < self.nz) & (there >= 0) & (there < self.nz)
        ref = self.side(at * 2 + 1 - self.x)
        return ok, remote(ref, ref, self.ss.at[way, t], self.sr.at[way, t], there * 2 + self.x, self.own)

    def joined(self, way, t):
        sign = 1 - 2 * way
        at = self.z - sign * (t + 1)
        ok = (at >= 0) & (at < self.nz)
        ref = self.side(at * 2 + 1 - self.x)
        return ok, remote(ref, ref, self.ss.at[way, t], self.sr.at[way, t], self.z * 2 + 1 - self.x, self.own)

    def start(self):
        for way in range(2):
            ok, copy = self.along(way, 0)
            pl.when(ok)(copy.start)
        self.across(0, 0)[1].start()

    def step(self, t):
        if t == 0:
            self.crossed(0, 0)[1].wait_recv()
            for way in range(2):
                ok, copy = self.aside(way, 0)
                pl.when(ok)(copy.start)
        for way in range(2):
            ok, copy = self.came(way, t)
            pl.when(ok)(copy.wait_recv)
            if t + 1 < self.nz - 1:
                ok, copy = self.along(way, t + 1)
                pl.when(ok)(copy.start)
            ok, copy = self.across(way, t + 1)
            pl.when(ok)(copy.start)
            if t > 0:
                self.joining(way, t - 1)

    def joining(self, way, t):
        ok, copy = self.joined(way, t)
        pl.when(ok)(copy.wait_recv)
        if t + 1 < self.nz - 1:
            ok, copy = self.aside(way, t + 1)
            pl.when(ok)(copy.start)

    def finish(self):
        for way in range(2):
            self.joining(way, self.nz - 2)
        for t in range(self.nz):
            for way in range(1 if t == 0 else 2):
                if t > 0:
                    ok, copy = self.crossed(way, t)
                    pl.when(ok)(copy.wait_recv)
                ok, copy = self.across(way, t)
                pl.when(ok)(copy.wait_send)
        for t in range(self.nz - 1):
            for way in range(2):
                ok, copy = self.along(way, t)
                pl.when(ok)(copy.wait_send)
                ok, copy = self.aside(way, t)
                pl.when(ok)(copy.wait_send)


def exchange_kernel(
    dps, owns, blocks, slots, part,
    pick, grad, root, whole, roots,
    halves, sums, landed, packed, x_send, x_recv, p_send, p_recv, o_send, o_recv,
    gzs, gzr, gxs, gxr, gss, gsr, rzs, rzr, rxs, rxr, rss, rsr, own_sem,
):
    dp, own = lax.axis_index("dp"), lax.axis_index("own")
    nz = dps // 2
    mine = pltpu.make_async_copy(root, roots.at[:, dp], own_sem)
    mine.start()
    greet(dps, owns)

    z, x = dp // 2, lax.rem(dp, 2)

    def chunk(at):
        return pl.ds(pl.multiple_of(at * part, part), part)

    def pair(k):
        there = lax.rem(z + k, nz)
        rows = chunk(there * 2 + 1 - x)
        return remote(grad.at[:, rows, :], halves.at[k], x_send.at[k], x_recv.at[k], z * 2 + 1 - x, own)

    def scatter(k):
        there = lax.rem(z + k, nz) * 2 + x
        return remote(sums.at[k - 1], landed.at[k - 1], p_send.at[k - 1], p_recv.at[k - 1], there, own)

    order = [nz // 2] + [k for k in range(1, nz) if k != nz // 2] + [0]
    for k in order:
        pair(k).start()
    mine.wait()
    height = root.shape[1]
    quarter = height // 4
    fetch = Gather(
        lambda at: roots.at[:, at],
        lambda at: roots.at[:, at, pl.ds(quarter, height - quarter)],
        lambda at: roots.at[:, at, pl.ds(0, quarter)],
        nz,
        (rzs, rzr, rxs, rxr, rss, rsr),
    )
    fetch.start()
    for k in order[:-1]:
        pair(k).wait_recv()
        rows = chunk(lax.rem(z + k, nz) * 2 + x)
        for b in range(blocks):
            total = grad[b, rows, :].astype(jnp.float32) + halves[k, b].astype(jnp.float32)
            sums[k - 1, b] = total.astype(jnp.bfloat16)
        scatter(k).start()
    for t in range(nz - 2):
        fetch.step(t)
    pair(0).wait_recv()
    for k in range(1, nz):
        scatter(k).wait_recv()
    rows = chunk(dp)
    for b in range(blocks):
        total = grad[b, rows, :].astype(jnp.float32) + halves[0, b].astype(jnp.float32)
        for k in range(1, nz):
            total = total + landed[k - 1, b].astype(jnp.float32)
        packed[owns * slots + b] = total.astype(jnp.bfloat16)
    for s in range(owns * slots):
        total = pick[s] * packed[owns * slots].astype(jnp.float32)
        for b in range(1, blocks):
            total = total + pick[b * owns * slots + s] * packed[owns * slots + b].astype(jnp.float32)
        packed[s] = total.astype(jnp.bfloat16)

    def deliver(k):
        there = lax.rem(own + k, owns)
        return remote(
            packed.at[pl.ds(there * slots, slots)], whole.at[:, own, dp], o_send.at[k - 1], o_recv.at[k - 1], dp, there
        )

    def delivered(k):
        source = lax.rem(own + owns - k, owns)
        return remote(
            packed.at[pl.ds(own * slots, slots)], whole.at[:, source, dp], o_send.at[k - 1], o_recv.at[k - 1], dp, lax.rem(own + k, owns)
        )

    for k in range(1, owns):
        deliver(k).start()
    for s in range(slots):
        whole[s, own, dp] = packed[own * slots + s]
    fetch.step(nz - 2)
    for k in range(1, owns):
        delivered(k).wait_recv()
    spread = Gather(
        lambda at: whole.at[:, :, at],
        lambda at: whole.at[:, pl.ds(1, owns - 1), at],
        lambda at: whole.at[:, 0, at],
        nz,
        (gzs, gzr, gxs, gxr, gss, gsr),
    )
    spread.start()
    for t in range(nz - 1):
        spread.step(t)
    fetch.finish()
    spread.finish()
    for k in range(1, owns):
        deliver(k).wait_send()
    for k in range(1, nz):
        scatter(k).wait_send()
    for k in range(nz):
        pair(k).wait_send()


def exchange(pick, grad, root, dps, owns):
    blocks, rows, cols = grad.shape
    slots, rows_dev = root.shape[:2]
    part = rows // dps
    nz = dps // 2
    dma = pltpu.SemaphoreType.DMA
    return pl.pallas_call(
        functools.partial(exchange_kernel, dps, owns, blocks, slots, part),
        out_shape=(
            jax.ShapeDtypeStruct((slots, owns, dps, part, cols), jnp.bfloat16),
            jax.ShapeDtypeStruct((slots, dps, rows_dev, cols), jnp.bfloat16),
        ),
        in_specs=[pl.BlockSpec(memory_space=pltpu.SMEM)] + [pl.BlockSpec(memory_space=VM)] * 2,
        out_specs=(pl.BlockSpec(memory_space=VM),) * 2,
        scratch_shapes=[
            VM((nz, blocks, part, cols), jnp.bfloat16),
            VM((nz - 1, blocks, part, cols), jnp.bfloat16),
            VM((nz - 1, blocks, part, cols), jnp.bfloat16),
            VM((owns * slots + blocks, part, cols), jnp.bfloat16),
            dma((nz,)),
            dma((nz,)),
            dma((nz - 1,)),
            dma((nz - 1,)),
            dma((owns - 1,)),
            dma((owns - 1,)),
        ]
        + [dma((2, nz))] * 12
        + [dma],
        compiler_params=pltpu.CompilerParams(collective_id=0, has_side_effects=True, vmem_limit_bytes=40 * MIB),
    )(pick, grad, root)


def finish_kernel(dps, owns, slots, part, squares, direction, master, sums, out, held, shares, s_send, s_recv, w_send, w_recv):
    dp, own = lax.axis_index("dp"), lax.axis_index("own")
    greet(dps, owns)

    def tell(k):
        return remote(squares, held.at[k - 1], s_send.at[k - 1], s_recv.at[k - 1], lax.rem(dp + k, dps), own)

    for k in range(1, dps):
        tell(k).start()
    for k in range(1, dps):
        tell(k).wait_recv()
    total = squares[...]
    for k in range(1, dps):
        total = total + held[k - 1]
    sums[...] = total
    for s in range(slots):
        graft = jnp.sqrt(total[s : s + 1, :1]) / (jnp.sqrt(total[slots + s : slots + s + 1, :1]) + 1e-06)
        for o in range(owns):
            rows = pl.ds(o * part, part)
            shares[o, s] = (master[s, rows, :] - learn_rate * graft * direction[s, rows, :]).astype(jnp.bfloat16)

    def deliver(k):
        there = lax.rem(own + k, owns)
        return remote(shares.at[there], out.at[own], w_send.at[k - 1], w_recv.at[k - 1], dp, there)

    def delivered(k):
        source = lax.rem(own + owns - k, owns)
        return remote(shares.at[own], out.at[source], w_send.at[k - 1], w_recv.at[k - 1], dp, lax.rem(own + k, owns))

    for k in range(1, owns):
        deliver(k).start()
    out[own] = shares[own]
    for k in range(1, owns):
        delivered(k).wait_recv()
    for k in range(1, owns):
        deliver(k).wait_send()
    for k in range(1, dps):
        tell(k).wait_send()


def finish(squares, direction, master, dps, owns):
    slots, rows_dev, cols = master.shape
    part = rows_dev // owns
    dma = pltpu.SemaphoreType.DMA
    return pl.pallas_call(
        functools.partial(finish_kernel, dps, owns, slots, part),
        out_shape=(
            jax.ShapeDtypeStruct(squares.shape, jnp.float32),
            jax.ShapeDtypeStruct((owns, slots, part, cols), jnp.bfloat16),
        ),
        in_specs=[pl.BlockSpec(memory_space=VM)] * 3,
        out_specs=(pl.BlockSpec(memory_space=VM),) * 2,
        scratch_shapes=[
            VM((dps - 1,) + squares.shape, jnp.float32),
            VM((owns, slots, part, cols), jnp.bfloat16),
            dma((dps - 1,)),
            dma((dps - 1,)),
            dma((owns - 1,)),
            dma((owns - 1,)),
        ],
        compiler_params=pltpu.CompilerParams(collective_id=1, has_side_effects=True, vmem_limit_bytes=24 * MIB),
    )(squares, direction, master)


def whole_by_collectives(grads, owner_map, root_right, occupied, block_of):
    owners = lax.axis_size("own")
    slot_count, _, order_size = root_right.shape
    summed = lax.psum(grads[0], "dp")
    packed = jnp.stack(
        [lax.dynamic_index_in_dim(summed, block_of[s], 0, keepdims=False) for s in range(owners * slot_count)]
    )
    packed = jnp.where(occupied[:, None, None], packed, 0.0)
    packed = packed.reshape(owners, slot_count, summed.shape[1], order_size).astype(jnp.bfloat16)
    arrived = lax.all_to_all(packed, "own", split_axis=0, concat_axis=2, tiled=True)
    return (
        arrived.reshape(slot_count, order_size, order_size),
        lax.all_gather(root_right, "dp", axis=1, tiled=True),
    )


def per_device(
    grads,
    owner_map,
    stat_left,
    stat_right,
    root_left,
    root_right,
    master,
    moment_first,
    moment_second,
):
    owners, groups = lax.axis_size("own"), lax.axis_size("dp")
    slot_count, rows_dev, order_size = stat_left.shape
    blocks = owner_map.shape[0]
    owned_slots = owners * slot_count
    matches = owner_map[:, None] == jnp.arange(owned_slots, dtype=jnp.int32)[None, :]
    occupied = jnp.any(matches, axis=0)
    kernels = groups % 2 == 0 and (grads.shape[2] // groups) % 16 == 0 and (rows_dev // owners) % 16 == 0 and rows_dev % 64 == 0
    if kernels:
        pick = matches.astype(jnp.float32).reshape(-1)
        whole, right = exchange(pick, grads[0].astype(jnp.bfloat16), root_right, groups, owners)
        whole = whole.reshape(slot_count, order_size, order_size)
        right = right.reshape(slot_count, order_size, order_size)
    else:
        block_of = jnp.sum(jnp.where(matches, jnp.arange(blocks, dtype=jnp.int32)[:, None], 0), axis=0)
        whole, right = whole_by_collectives(grads, owner_map, root_right, occupied, block_of)
    first_row = lax.axis_index("dp") * rows_dev
    own_rows = lax.dynamic_slice_in_dim(whole, first_row, rows_dev, 1)
    own_cols = lax.dynamic_slice_in_dim(whole, first_row, rows_dev, 2)
    mixed = jnp.einsum("srk,skn->srn", root_left, whole, preferred_element_type=jnp.float32)
    direction = jnp.einsum(
        "srk,skn->srn", mixed.astype(jnp.bfloat16), right, preferred_element_type=jnp.float32
    )
    rows32 = own_rows.astype(jnp.float32)
    first_new = first_decay * moment_first + (1.0 - first_decay) * rows32
    second_new = second_decay * moment_second + (1.0 - second_decay) * rows32 * rows32
    adam_step = first_new / (jnp.sqrt(second_new) + 1e-08)
    square_sums = jnp.concatenate(
        [jnp.sum(adam_step * adam_step, axis=(1, 2)), jnp.sum(direction * direction, axis=(1, 2))]
    )
    if kernels:
        padded = jnp.pad(square_sums, (0, -2 * slot_count % 8))
        totals, delivered = finish(
            jnp.broadcast_to(padded[:, None], (padded.shape[0], 128)), direction, master, groups, owners
        )
        square_sums = totals[: 2 * slot_count, 0]
    else:
        square_sums = lax.psum(square_sums, "dp")
    graft = jnp.sqrt(square_sums[:slot_count]) / (jnp.sqrt(square_sums[slot_count:]) + 1e-06)
    master_new = master - learn_rate * graft[:, None, None] * direction
    if not kernels:
        shares = master_new.astype(jnp.bfloat16).reshape(slot_count, owners, rows_dev // owners, order_size)
        delivered = lax.all_to_all(shares, "own", split_axis=1, concat_axis=0, tiled=True)
    delivered = delivered.reshape(owned_slots, rows_dev // owners, order_size)
    left_new = stat_decay * stat_left + (1.0 - stat_decay) * jnp.einsum(
        "srk,snk->srn", own_rows, whole, preferred_element_type=jnp.float32
    )
    right_new = stat_decay * stat_right + (1.0 - stat_decay) * jnp.einsum(
        "skr,skn->srn", own_cols, whole, preferred_element_type=jnp.float32
    )
    occupied_mine = lax.dynamic_slice_in_dim(
        occupied, lax.axis_index("own") * slot_count, slot_count
    )[:, None, None]
    left_next = jnp.where(occupied_mine, left_new, stat_left)
    right_next = jnp.where(occupied_mine, right_new, stat_right)
    master_next = jnp.where(occupied_mine, master_new, master)
    first_next = jnp.where(occupied_mine, first_new, moment_first)
    second_next = jnp.where(occupied_mine, second_new, moment_second)
    weights_out = jnp.zeros((blocks,) + delivered.shape[1:], delivered.dtype)
    for s in range(owned_slots):
        weights_out = jnp.where(matches[:, s, None, None], delivered[s][None], weights_out)
    return (left_next, right_next, master_next, first_next, second_next, weights_out)


def solution(mesh):
    state = P("own", "dp", None)
    return jax.shard_map(
        per_device,
        mesh=mesh,
        in_specs=(P("dp", None, "own", None), P()) + (state,) * 7,
        out_specs=(state,) * 5 + (P(None, ("dp", "own"), None),),
        check_vma=False,
    )
```

```python
import functools

import jax
import jax.numpy as jnp
from jax import lax
from jax.experimental import pallas as pl
from jax.experimental.pallas import tpu as pltpu
from jax.sharding import PartitionSpec as P

stat_decay = 0.9
first_decay = 0.9
second_decay = 0.99
learn_rate = 0.25

VM = pltpu.VMEM
MIB = 1 << 20


def remote(src, dst, send, recv, dp, own):
    return pltpu.make_async_remote_copy(
        src_ref=src,
        dst_ref=dst,
        send_sem=send,
        recv_sem=recv,
        device_id=(dp, own),
        device_id_type=pl.DeviceIdType.MESH,
    )


def greet(dps, owns):
    dp, own = lax.axis_index("dp"), lax.axis_index("own")
    barrier = pltpu.get_barrier_semaphore()
    for k in range(1, dps):
        pl.semaphore_signal(barrier, inc=1, device_id=(lax.rem(dp + k, dps), own), device_id_type=pl.DeviceIdType.MESH)
    for k in range(1, owns):
        pl.semaphore_signal(barrier, inc=1, device_id=(dp, lax.rem(own + k, owns)), device_id_type=pl.DeviceIdType.MESH)
    pl.semaphore_wait(barrier, dps + owns - 2)


class Gather:
    def __init__(self, piece, main, side, nz, sems):
        self.piece, self.main, self.side, self.nz = piece, main, side, nz
        self.zs, self.zr, self.xs, self.xr, self.ss, self.sr = sems
        dp = lax.axis_index("dp")
        self.own = lax.axis_index("own")
        self.z, self.x = dp // 2, lax.rem(dp, 2)

    def along(self, way, t):
        sign = 1 - 2 * way
        at = self.z - sign * t
        there = self.z + sign
        ok = (at >= 0) & (at < self.nz) & (there >= 0) & (there < self.nz)
        ref = self.piece(at * 2 + self.x)
        return ok, remote(ref, ref, self.zs.at[way, t], self.zr.at[way, t], there * 2 + self.x, self.own)

    def across(self, way, t):
        sign = 1 - 2 * way
        at = self.z - sign * t
        ok = (at >= 0) & (at < self.nz)
        ref = (self.main if t else self.piece)(at * 2 + self.x)
        return ok, remote(ref, ref, self.xs.at[way, t], self.xr.at[way, t], self.z * 2 + 1 - self.x, self.own)

    def came(self, way, t):
        sign = 1 - 2 * way
        at = self.z - sign * (t + 1)
        ok = (at >= 0) & (at < self.nz)
        ref = self.piece(at * 2 + self.x)
        return ok, remote(ref, ref, self.zs.at[way, t], self.zr.at[way, t], self.z * 2 + 1 - self.x, self.own)

    def crossed(self, way, t):
        sign = 1 - 2 * way
        at = self.z - sign * t
        ok = (at >= 0) & (at < self.nz)
        ref = (self.main if t else self.piece)(at * 2 + 1 - self.x)
        return ok, remote(ref, ref, self.xs.at[way, t], self.xr.at[way, t], self.z * 2 + 1 - self.x, self.own)

    def aside(self, way, t):
        sign = 1 - 2 * way
        at = self.z - sign * t
        there = self.z + sign
        ok = (at >= 0) & (at < self.nz) & (there >= 0) & (there < self.nz)
        ref = self.side(at * 2 + 1 - self.x)
        return ok, remote(ref, ref, self.ss.at[way, t], self.sr.at[way, t], there * 2 + self.x, self.own)

    def joined(self, way, t):
        sign = 1 - 2 * way
        at = self.z - sign * (t + 1)
        ok = (at >= 0) & (at < self.nz)
        ref = self.side(at * 2 + 1 - self.x)
        return ok, remote(ref, ref, self.ss.at[way, t], self.sr.at[way, t], self.z * 2 + 1 - self.x, self.own)

    def start(self):
        for way in range(2):
            ok, copy = self.along(way, 0)
            pl.when(ok)(copy.start)
        self.across(0, 0)[1].start()

    def step(self, t):
        if t == 0:
            self.crossed(0, 0)[1].wait_recv()
            for way in range(2):
                ok, copy = self.aside(way, 0)
                pl.when(ok)(copy.start)
        for way in range(2):
            ok, copy = self.came(way, t)
            pl.when(ok)(copy.wait_recv)
            if t + 1 < self.nz - 1:
                ok, copy = self.along(way, t + 1)
                pl.when(ok)(copy.start)
            ok, copy = self.across(way, t + 1)
            pl.when(ok)(copy.start)
            if t > 0:
                self.joining(way, t - 1)

    def joining(self, way, t):
        ok, copy = self.joined(way, t)
        pl.when(ok)(copy.wait_recv)
        if t + 1 < self.nz - 1:
            ok, copy = self.aside(way, t + 1)
            pl.when(ok)(copy.start)

    def finish(self):
        for way in range(2):
            self.joining(way, self.nz - 2)
        for t in range(self.nz):
            for way in range(1 if t == 0 else 2):
                if t > 0:
                    ok, copy = self.crossed(way, t)
                    pl.when(ok)(copy.wait_recv)
                ok, copy = self.across(way, t)
                pl.when(ok)(copy.wait_send)
        for t in range(self.nz - 1):
            for way in range(2):
                ok, copy = self.along(way, t)
                pl.when(ok)(copy.wait_send)
                ok, copy = self.aside(way, t)
                pl.when(ok)(copy.wait_send)


def exchange_kernel(
    dps, owns, blocks, slots, part,
    pick, grad, root, whole, roots,
    halves, sums, landed, packed, x_send, x_recv, p_send, p_recv, o_send, o_recv,
    gzs, gzr, gxs, gxr, gss, gsr, rzs, rzr, rxs, rxr, rss, rsr, own_sem,
):
    dp, own = lax.axis_index("dp"), lax.axis_index("own")
    nz = dps // 2
    mine = pltpu.make_async_copy(root, roots.at[:, dp], own_sem)
    mine.start()
    greet(dps, owns)

    z, x = dp // 2, lax.rem(dp, 2)

    def chunk(at):
        return pl.ds(pl.multiple_of(at * part, part), part)

    def pair(k):
        there = lax.rem(z + k, nz)
        rows = chunk(there * 2 + 1 - x)
        return remote(grad.at[:, rows, :], halves.at[k], x_send.at[k], x_recv.at[k], z * 2 + 1 - x, own)

    def scatter(k):
        there = lax.rem(z + k, nz) * 2 + x
        return remote(sums.at[k - 1], landed.at[k - 1], p_send.at[k - 1], p_recv.at[k - 1], there, own)

    order = [nz // 2] + [k for k in range(1, nz) if k != nz // 2] + [0]
    for k in order:
        pair(k).start()
    mine.wait()
    height = root.shape[1]
    quarter = height // 4
    fetch = Gather(
        lambda at: roots.at[:, at],
        lambda at: roots.at[:, at, pl.ds(quarter, height - quarter)],
        lambda at: roots.at[:, at, pl.ds(0, quarter)],
        nz,
        (rzs, rzr, rxs, rxr, rss, rsr),
    )
    fetch.start()
    for k in order[:-1]:
        pair(k).wait_recv()
        rows = chunk(lax.rem(z + k, nz) * 2 + x)
        for b in range(blocks):
            total = grad[b, rows, :].astype(jnp.float32) + halves[k, b].astype(jnp.float32)
            sums[k - 1, b] = total.astype(jnp.bfloat16)
        scatter(k).start()
    for t in range(nz - 2):
        fetch.step(t)
    pair(0).wait_recv()
    for k in range(1, nz):
        scatter(k).wait_recv()
    rows = chunk(dp)
    for b in range(blocks):
        total = grad[b, rows, :].astype(jnp.float32) + halves[0, b].astype(jnp.float32)
        for k in range(1, nz):
            total = total + landed[k - 1, b].astype(jnp.float32)
        packed[owns * slots + b] = total.astype(jnp.bfloat16)
    for s in range(owns * slots):
        total = pick[s] * packed[owns * slots].astype(jnp.float32)
        for b in range(1, blocks):
            total = total + pick[b * owns * slots + s] * packed[owns * slots + b].astype(jnp.float32)
        packed[s] = total.astype(jnp.bfloat16)

    def deliver(k):
        there = lax.rem(own + k, owns)
        return remote(
            packed.at[pl.ds(there * slots, slots)], whole.at[:, own, dp], o_send.at[k - 1], o_recv.at[k - 1], dp, there
        )

    def delivered(k):
        source = lax.rem(own + owns - k, owns)
        return remote(
            packed.at[pl.ds(own * slots, slots)], whole.at[:, source, dp], o_send.at[k - 1], o_recv.at[k - 1], dp, lax.rem(own + k, owns)
        )

    for k in range(1, owns):
        deliver(k).start()
    kept = pltpu.make_async_copy(packed.at[pl.ds(own * slots, slots)], whole.at[:, own, dp], own_sem)
    kept.start()
    fetch.step(nz - 2)
    kept.wait()
    for k in range(1, owns):
        delivered(k).wait_recv()
    spread = Gather(
        lambda at: whole.at[:, :, at],
        lambda at: whole.at[:, pl.ds(1, owns - 1), at],
        lambda at: whole.at[:, 0, at],
        nz,
        (gzs, gzr, gxs, gxr, gss, gsr),
    )
    spread.start()
    for t in range(nz - 1):
        spread.step(t)
    fetch.finish()
    spread.finish()
    for k in range(1, owns):
        deliver(k).wait_send()
    for k in range(1, nz):
        scatter(k).wait_send()
    for k in range(nz):
        pair(k).wait_send()


def exchange(pick, grad, root, dps, owns):
    blocks, rows, cols = grad.shape
    slots, rows_dev = root.shape[:2]
    part = rows // dps
    nz = dps // 2
    dma = pltpu.SemaphoreType.DMA
    return pl.pallas_call(
        functools.partial(exchange_kernel, dps, owns, blocks, slots, part),
        out_shape=(
            jax.ShapeDtypeStruct((slots, owns, dps, part, cols), jnp.bfloat16),
            jax.ShapeDtypeStruct((slots, dps, rows_dev, cols), jnp.bfloat16),
        ),
        in_specs=[pl.BlockSpec(memory_space=pltpu.SMEM)] + [pl.BlockSpec(memory_space=VM)] * 2,
        out_specs=(pl.BlockSpec(memory_space=pltpu.HBM),) * 2,
        scratch_shapes=[
            VM((nz, blocks, part, cols), jnp.bfloat16),
            VM((nz - 1, blocks, part, cols), jnp.bfloat16),
            VM((nz - 1, blocks, part, cols), jnp.bfloat16),
            VM((owns * slots + blocks, part, cols), jnp.bfloat16),
            dma((nz,)),
            dma((nz,)),
            dma((nz - 1,)),
            dma((nz - 1,)),
            dma((owns - 1,)),
            dma((owns - 1,)),
        ]
        + [dma((2, nz))] * 12
        + [dma],
        compiler_params=pltpu.CompilerParams(collective_id=0, has_side_effects=True, vmem_limit_bytes=56 * MIB),
    )(pick, grad, root)


def finish_kernel(dps, owns, slots, part, squares, direction, master, sums, out, held, shares, s_send, s_recv, w_send, w_recv):
    dp, own = lax.axis_index("dp"), lax.axis_index("own")
    greet(dps, owns)

    def tell(k):
        return remote(squares, held.at[k - 1], s_send.at[k - 1], s_recv.at[k - 1], lax.rem(dp + k, dps), own)

    for k in range(1, dps):
        tell(k).start()
    for k in range(1, dps):
        tell(k).wait_recv()
    total = squares[...]
    for k in range(1, dps):
        total = total + held[k - 1]
    sums[...] = total
    for s in range(slots):
        graft = jnp.sqrt(total[s : s + 1, :1]) / (jnp.sqrt(total[slots + s : slots + s + 1, :1]) + 1e-06)
        for o in range(owns):
            rows = pl.ds(o * part, part)
            shares[o, s] = (master[s, rows, :] - learn_rate * graft * direction[s, rows, :]).astype(jnp.bfloat16)

    def deliver(k):
        there = lax.rem(own + k, owns)
        return remote(shares.at[there], out.at[own], w_send.at[k - 1], w_recv.at[k - 1], dp, there)

    def delivered(k):
        source = lax.rem(own + owns - k, owns)
        return remote(shares.at[own], out.at[source], w_send.at[k - 1], w_recv.at[k - 1], dp, lax.rem(own + k, owns))

    for k in range(1, owns):
        deliver(k).start()
    out[own] = shares[own]
    for k in range(1, owns):
        delivered(k).wait_recv()
    for k in range(1, owns):
        deliver(k).wait_send()
    for k in range(1, dps):
        tell(k).wait_send()


def finish(squares, direction, master, dps, owns):
    slots, rows_dev, cols = master.shape
    part = rows_dev // owns
    dma = pltpu.SemaphoreType.DMA
    return pl.pallas_call(
        functools.partial(finish_kernel, dps, owns, slots, part),
        out_shape=(
            jax.ShapeDtypeStruct(squares.shape, jnp.float32),
            jax.ShapeDtypeStruct((owns, slots, part, cols), jnp.bfloat16),
        ),
        in_specs=[pl.BlockSpec(memory_space=VM)] * 3,
        out_specs=(pl.BlockSpec(memory_space=VM),) * 2,
        scratch_shapes=[
            VM((dps - 1,) + squares.shape, jnp.float32),
            VM((owns, slots, part, cols), jnp.bfloat16),
            dma((dps - 1,)),
            dma((dps - 1,)),
            dma((owns - 1,)),
            dma((owns - 1,)),
        ],
        compiler_params=pltpu.CompilerParams(collective_id=1, has_side_effects=True, vmem_limit_bytes=24 * MIB),
    )(squares, direction, master)


def whole_by_collectives(grads, owner_map, root_right, occupied, block_of):
    owners = lax.axis_size("own")
    slot_count, _, order_size = root_right.shape
    summed = lax.psum(grads[0], "dp")
    packed = jnp.stack(
        [lax.dynamic_index_in_dim(summed, block_of[s], 0, keepdims=False) for s in range(owners * slot_count)]
    )
    packed = jnp.where(occupied[:, None, None], packed, 0.0)
    packed = packed.reshape(owners, slot_count, summed.shape[1], order_size).astype(jnp.bfloat16)
    arrived = lax.all_to_all(packed, "own", split_axis=0, concat_axis=2, tiled=True)
    return (
        arrived.reshape(slot_count, order_size, order_size),
        lax.all_gather(root_right, "dp", axis=1, tiled=True),
    )


def per_device(
    grads,
    owner_map,
    stat_left,
    stat_right,
    root_left,
    root_right,
    master,
    moment_first,
    moment_second,
):
    owners, groups = lax.axis_size("own"), lax.axis_size("dp")
    slot_count, rows_dev, order_size = stat_left.shape
    blocks = owner_map.shape[0]
    owned_slots = owners * slot_count
    matches = owner_map[:, None] == jnp.arange(owned_slots, dtype=jnp.int32)[None, :]
    occupied = jnp.any(matches, axis=0)
    kernels = groups % 2 == 0 and (grads.shape[2] // groups) % 16 == 0 and (rows_dev // owners) % 16 == 0 and rows_dev % 64 == 0
    if kernels:
        pick = matches.astype(jnp.float32).reshape(-1)
        whole, right = exchange(pick, grads[0].astype(jnp.bfloat16), root_right, groups, owners)
        whole = whole.reshape(slot_count, order_size, order_size)
        right = right.reshape(slot_count, order_size, order_size)
    else:
        block_of = jnp.sum(jnp.where(matches, jnp.arange(blocks, dtype=jnp.int32)[:, None], 0), axis=0)
        whole, right = whole_by_collectives(grads, owner_map, root_right, occupied, block_of)
    first_row = lax.axis_index("dp") * rows_dev
    own_rows = lax.dynamic_slice_in_dim(whole, first_row, rows_dev, 1)
    own_cols = lax.dynamic_slice_in_dim(whole, first_row, rows_dev, 2)
    mixed = jnp.einsum("srk,skn->srn", root_left, whole, preferred_element_type=jnp.float32)
    direction = jnp.einsum(
        "srk,skn->srn", mixed.astype(jnp.bfloat16), right, preferred_element_type=jnp.float32
    )
    rows32 = own_rows.astype(jnp.float32)
    first_new = first_decay * moment_first + (1.0 - first_decay) * rows32
    second_new = second_decay * moment_second + (1.0 - second_decay) * rows32 * rows32
    adam_step = first_new / (jnp.sqrt(second_new) + 1e-08)
    square_sums = jnp.concatenate(
        [jnp.sum(adam_step * adam_step, axis=(1, 2)), jnp.sum(direction * direction, axis=(1, 2))]
    )
    if kernels:
        padded = jnp.pad(square_sums, (0, -2 * slot_count % 8))
        totals, delivered = finish(
            jnp.broadcast_to(padded[:, None], (padded.shape[0], 128)), direction, master, groups, owners
        )
        square_sums = totals[: 2 * slot_count, 0]
    else:
        square_sums = lax.psum(square_sums, "dp")
    graft = jnp.sqrt(square_sums[:slot_count]) / (jnp.sqrt(square_sums[slot_count:]) + 1e-06)
    master_new = master - learn_rate * graft[:, None, None] * direction
    if not kernels:
        shares = master_new.astype(jnp.bfloat16).reshape(slot_count, owners, rows_dev // owners, order_size)
        delivered = lax.all_to_all(shares, "own", split_axis=1, concat_axis=0, tiled=True)
    delivered = delivered.reshape(owned_slots, rows_dev // owners, order_size)
    left_new = stat_decay * stat_left + (1.0 - stat_decay) * jnp.einsum(
        "srk,snk->srn", own_rows, whole, preferred_element_type=jnp.float32
    )
    right_new = stat_decay * stat_right + (1.0 - stat_decay) * jnp.einsum(
        "skr,skn->srn", own_cols, whole, preferred_element_type=jnp.float32
    )
    occupied_mine = lax.dynamic_slice_in_dim(
        occupied, lax.axis_index("own") * slot_count, slot_count
    )[:, None, None]
    left_next = jnp.where(occupied_mine, left_new, stat_left)
    right_next = jnp.where(occupied_mine, right_new, stat_right)
    master_next = jnp.where(occupied_mine, master_new, master)
    first_next = jnp.where(occupied_mine, first_new, moment_first)
    second_next = jnp.where(occupied_mine, second_new, moment_second)
    weights_out = jnp.zeros((blocks,) + delivered.shape[1:], delivered.dtype)
    for s in range(owned_slots):
        weights_out = jnp.where(matches[:, s, None, None], delivered[s][None], weights_out)
    return (left_next, right_next, master_next, first_next, second_next, weights_out)


def solution(mesh):
    state = P("own", "dp", None)
    return jax.shard_map(
        per_device,
        mesh=mesh,
        in_specs=(P("dp", None, "own", None), P()) + (state,) * 7,
        out_specs=(state,) * 5 + (P(None, ("dp", "own"), None),),
        check_vma=False,
    )
```

```python
import functools

import jax
import jax.numpy as jnp
from jax import lax
from jax.experimental import pallas as pl
from jax.experimental.pallas import tpu as pltpu
from jax.sharding import PartitionSpec as P

stat_decay = 0.9
first_decay = 0.9
second_decay = 0.99
learn_rate = 0.25

VM = pltpu.VMEM
MIB = 1 << 20


def remote(src, dst, send, recv, dp, own):
    return pltpu.make_async_remote_copy(
        src_ref=src,
        dst_ref=dst,
        send_sem=send,
        recv_sem=recv,
        device_id=(dp, own),
        device_id_type=pl.DeviceIdType.MESH,
    )


def greet(dps, owns):
    dp, own = lax.axis_index("dp"), lax.axis_index("own")
    barrier = pltpu.get_barrier_semaphore()
    for k in range(1, dps):
        pl.semaphore_signal(barrier, inc=1, device_id=(lax.rem(dp + k, dps), own), device_id_type=pl.DeviceIdType.MESH)
    for k in range(1, owns):
        pl.semaphore_signal(barrier, inc=1, device_id=(dp, lax.rem(own + k, owns)), device_id_type=pl.DeviceIdType.MESH)
    pl.semaphore_wait(barrier, dps + owns - 2)


class Gather:
    def __init__(self, piece, main, side, nz, sems):
        self.piece, self.main, self.side, self.nz = piece, main, side, nz
        self.zs, self.zr, self.xs, self.xr, self.ss, self.sr = sems
        dp = lax.axis_index("dp")
        self.own = lax.axis_index("own")
        self.z, self.x = dp // 2, lax.rem(dp, 2)

    def along(self, way, t):
        sign = 1 - 2 * way
        at = self.z - sign * t
        there = self.z + sign
        ok = (at >= 0) & (at < self.nz) & (there >= 0) & (there < self.nz)
        ref = self.piece(at * 2 + self.x)
        return ok, remote(ref, ref, self.zs.at[way, t], self.zr.at[way, t], there * 2 + self.x, self.own)

    def across(self, way, t):
        sign = 1 - 2 * way
        at = self.z - sign * t
        ok = (at >= 0) & (at < self.nz)
        ref = (self.main if t else self.piece)(at * 2 + self.x)
        return ok, remote(ref, ref, self.xs.at[way, t], self.xr.at[way, t], self.z * 2 + 1 - self.x, self.own)

    def came(self, way, t):
        sign = 1 - 2 * way
        at = self.z - sign * (t + 1)
        ok = (at >= 0) & (at < self.nz)
        ref = self.piece(at * 2 + self.x)
        return ok, remote(ref, ref, self.zs.at[way, t], self.zr.at[way, t], self.z * 2 + 1 - self.x, self.own)

    def crossed(self, way, t):
        sign = 1 - 2 * way
        at = self.z - sign * t
        ok = (at >= 0) & (at < self.nz)
        ref = (self.main if t else self.piece)(at * 2 + 1 - self.x)
        return ok, remote(ref, ref, self.xs.at[way, t], self.xr.at[way, t], self.z * 2 + 1 - self.x, self.own)

    def aside(self, way, t):
        sign = 1 - 2 * way
        at = self.z - sign * t
        there = self.z + sign
        ok = (at >= 0) & (at < self.nz) & (there >= 0) & (there < self.nz)
        ref = self.side(at * 2 + 1 - self.x)
        return ok, remote(ref, ref, self.ss.at[way, t], self.sr.at[way, t], there * 2 + self.x, self.own)

    def joined(self, way, t):
        sign = 1 - 2 * way
        at = self.z - sign * (t + 1)
        ok = (at >= 0) & (at < self.nz)
        ref = self.side(at * 2 + 1 - self.x)
        return ok, remote(ref, ref, self.ss.at[way, t], self.sr.at[way, t], self.z * 2 + 1 - self.x, self.own)

    def start(self):
        for way in range(2):
            ok, copy = self.along(way, 0)
            pl.when(ok)(copy.start)
        self.across(0, 0)[1].start()

    def step(self, t):
        if t == 0:
            self.crossed(0, 0)[1].wait_recv()
            for way in range(2):
                ok, copy = self.aside(way, 0)
                pl.when(ok)(copy.start)
        for way in range(2):
            ok, copy = self.came(way, t)
            pl.when(ok)(copy.wait_recv)
            if t + 1 < self.nz - 1:
                ok, copy = self.along(way, t + 1)
                pl.when(ok)(copy.start)
            ok, copy = self.across(way, t + 1)
            pl.when(ok)(copy.start)
            if t > 0:
                self.joining(way, t - 1)

    def joining(self, way, t):
        ok, copy = self.joined(way, t)
        pl.when(ok)(copy.wait_recv)
        if t + 1 < self.nz - 1:
            ok, copy = self.aside(way, t + 1)
            pl.when(ok)(copy.start)

    def finish(self):
        for way in range(2):
            self.joining(way, self.nz - 2)
        for t in range(self.nz):
            for way in range(1 if t == 0 else 2):
                if t > 0:
                    ok, copy = self.crossed(way, t)
                    pl.when(ok)(copy.wait_recv)
                ok, copy = self.across(way, t)
                pl.when(ok)(copy.wait_send)
        for t in range(self.nz - 1):
            for way in range(2):
                ok, copy = self.along(way, t)
                pl.when(ok)(copy.wait_send)
                ok, copy = self.aside(way, t)
                pl.when(ok)(copy.wait_send)


def exchange_kernel(
    dps, owns, blocks, slots, part,
    pick, grad, root, whole, roots,
    halves, sums, landed, packed, x_send, x_recv, p_send, p_recv, o_send, o_recv,
    gzs, gzr, gxs, gxr, gss, gsr, rzs, rzr, rxs, rxr, rss, rsr, own_sem,
):
    dp, own = lax.axis_index("dp"), lax.axis_index("own")
    nz = dps // 2
    mine = pltpu.make_async_copy(root, roots.at[:, dp], own_sem)
    mine.start()
    greet(dps, owns)

    z, x = dp // 2, lax.rem(dp, 2)

    def chunk(at):
        return pl.ds(pl.multiple_of(at * part, part), part)

    def pair(k):
        there = lax.rem(z + k, nz)
        rows = chunk(there * 2 + 1 - x)
        return remote(grad.at[:, rows, :], halves.at[k], x_send.at[k], x_recv.at[k], z * 2 + 1 - x, own)

    def scatter(k):
        there = lax.rem(z + k, nz) * 2 + x
        return remote(sums.at[k - 1], landed.at[k - 1], p_send.at[k - 1], p_recv.at[k - 1], there, own)

    order = [nz // 2] + [k for k in range(1, nz) if k != nz // 2] + [0]
    for k in order:
        pair(k).start()
    mine.wait()
    height = root.shape[1]
    quarter = height // 4
    fetch = Gather(
        lambda at: roots.at[:, at],
        lambda at: roots.at[:, at, pl.ds(quarter, height - quarter)],
        lambda at: roots.at[:, at, pl.ds(0, quarter)],
        nz,
        (rzs, rzr, rxs, rxr, rss, rsr),
    )
    fetch.start()
    for k in order[:-1]:
        pair(k).wait_recv()
        rows = chunk(lax.rem(z + k, nz) * 2 + x)
        for b in range(blocks):
            total = grad[b, rows, :].astype(jnp.float32) + halves[k, b].astype(jnp.float32)
            sums[k - 1, b] = total.astype(jnp.bfloat16)
        scatter(k).start()
    fetch.step(0)
    pair(0).wait_recv()
    for k in range(1, nz):
        scatter(k).wait_recv()
    rows = chunk(dp)
    for b in range(blocks):
        total = grad[b, rows, :].astype(jnp.float32) + halves[0, b].astype(jnp.float32)
        for k in range(1, nz):
            total = total + landed[k - 1, b].astype(jnp.float32)
        packed[owns * slots + b] = total.astype(jnp.bfloat16)
    for s in range(owns * slots):
        total = pick[s] * packed[owns * slots].astype(jnp.float32)
        for b in range(1, blocks):
            total = total + pick[b * owns * slots + s] * packed[owns * slots + b].astype(jnp.float32)
        packed[s] = total.astype(jnp.bfloat16)

    def deliver(k):
        there = lax.rem(own + k, owns)
        return remote(
            packed.at[pl.ds(there * slots, slots)], whole.at[:, own, dp], o_send.at[k - 1], o_recv.at[k - 1], dp, there
        )

    def delivered(k):
        source = lax.rem(own + owns - k, owns)
        return remote(
            packed.at[pl.ds(own * slots, slots)], whole.at[:, source, dp], o_send.at[k - 1], o_recv.at[k - 1], dp, lax.rem(own + k, owns)
        )

    for k in range(1, owns):
        deliver(k).start()
    kept = pltpu.make_async_copy(packed.at[pl.ds(own * slots, slots)], whole.at[:, own, dp], own_sem)
    kept.start()
    kept.wait()
    for k in range(1, owns):
        delivered(k).wait_recv()
    spread = Gather(
        lambda at: whole.at[:, :, at],
        lambda at: whole.at[:, pl.ds(1, owns - 1), at],
        lambda at: whole.at[:, 0, at],
        nz,
        (gzs, gzr, gxs, gxr, gss, gsr),
    )
    spread.start()
    for t in range(nz - 1):
        if t > 0:
            fetch.step(t)
        spread.step(t)
    fetch.finish()
    spread.finish()
    for k in range(1, owns):
        deliver(k).wait_send()
    for k in range(1, nz):
        scatter(k).wait_send()
    for k in range(nz):
        pair(k).wait_send()


def exchange(pick, grad, root, dps, owns):
    blocks, rows, cols = grad.shape
    slots, rows_dev = root.shape[:2]
    part = rows // dps
    nz = dps // 2
    dma = pltpu.SemaphoreType.DMA
    return pl.pallas_call(
        functools.partial(exchange_kernel, dps, owns, blocks, slots, part),
        out_shape=(
            jax.ShapeDtypeStruct((slots, owns, dps, part, cols), jnp.bfloat16),
            jax.ShapeDtypeStruct((slots, dps, rows_dev, cols), jnp.bfloat16),
        ),
        in_specs=[pl.BlockSpec(memory_space=pltpu.SMEM)] + [pl.BlockSpec(memory_space=VM)] * 2,
        out_specs=(pl.BlockSpec(memory_space=pltpu.HBM),) * 2,
        scratch_shapes=[
            VM((nz, blocks, part, cols), jnp.bfloat16),
            VM((nz - 1, blocks, part, cols), jnp.bfloat16),
            VM((nz - 1, blocks, part, cols), jnp.bfloat16),
            VM((owns * slots + blocks, part, cols), jnp.bfloat16),
            dma((nz,)),
            dma((nz,)),
            dma((nz - 1,)),
            dma((nz - 1,)),
            dma((owns - 1,)),
            dma((owns - 1,)),
        ]
        + [dma((2, nz))] * 12
        + [dma],
        compiler_params=pltpu.CompilerParams(collective_id=0, has_side_effects=True, vmem_limit_bytes=56 * MIB),
    )(pick, grad, root)


def finish_kernel(dps, owns, slots, part, squares, direction, master, sums, out, held, shares, s_send, s_recv, w_send, w_recv):
    dp, own = lax.axis_index("dp"), lax.axis_index("own")
    greet(dps, owns)

    def tell(k):
        return remote(squares, held.at[k - 1], s_send.at[k - 1], s_recv.at[k - 1], lax.rem(dp + k, dps), own)

    for k in range(1, dps):
        tell(k).start()
    for k in range(1, dps):
        tell(k).wait_recv()
    total = squares[...]
    for k in range(1, dps):
        total = total + held[k - 1]
    sums[...] = total
    for s in range(slots):
        graft = jnp.sqrt(total[s : s + 1, :1]) / (jnp.sqrt(total[slots + s : slots + s + 1, :1]) + 1e-06)
        for o in range(owns):
            rows = pl.ds(o * part, part)
            shares[o, s] = (master[s, rows, :] - learn_rate * graft * direction[s, rows, :]).astype(jnp.bfloat16)

    def deliver(k):
        there = lax.rem(own + k, owns)
        return remote(shares.at[there], out.at[own], w_send.at[k - 1], w_recv.at[k - 1], dp, there)

    def delivered(k):
        source = lax.rem(own + owns - k, owns)
        return remote(shares.at[own], out.at[source], w_send.at[k - 1], w_recv.at[k - 1], dp, lax.rem(own + k, owns))

    for k in range(1, owns):
        deliver(k).start()
    out[own] = shares[own]
    for k in range(1, owns):
        delivered(k).wait_recv()
    for k in range(1, owns):
        deliver(k).wait_send()
    for k in range(1, dps):
        tell(k).wait_send()


def finish(squares, direction, master, dps, owns):
    slots, rows_dev, cols = master.shape
    part = rows_dev // owns
    dma = pltpu.SemaphoreType.DMA
    return pl.pallas_call(
        functools.partial(finish_kernel, dps, owns, slots, part),
        out_shape=(
            jax.ShapeDtypeStruct(squares.shape, jnp.float32),
            jax.ShapeDtypeStruct((owns, slots, part, cols), jnp.bfloat16),
        ),
        in_specs=[pl.BlockSpec(memory_space=VM)] * 3,
        out_specs=(pl.BlockSpec(memory_space=VM),) * 2,
        scratch_shapes=[
            VM((dps - 1,) + squares.shape, jnp.float32),
            VM((owns, slots, part, cols), jnp.bfloat16),
            dma((dps - 1,)),
            dma((dps - 1,)),
            dma((owns - 1,)),
            dma((owns - 1,)),
        ],
        compiler_params=pltpu.CompilerParams(collective_id=1, has_side_effects=True, vmem_limit_bytes=24 * MIB),
    )(squares, direction, master)


def whole_by_collectives(grads, owner_map, root_right, occupied, block_of):
    owners = lax.axis_size("own")
    slot_count, _, order_size = root_right.shape
    summed = lax.psum(grads[0], "dp")
    packed = jnp.stack(
        [lax.dynamic_index_in_dim(summed, block_of[s], 0, keepdims=False) for s in range(owners * slot_count)]
    )
    packed = jnp.where(occupied[:, None, None], packed, 0.0)
    packed = packed.reshape(owners, slot_count, summed.shape[1], order_size).astype(jnp.bfloat16)
    arrived = lax.all_to_all(packed, "own", split_axis=0, concat_axis=2, tiled=True)
    return (
        arrived.reshape(slot_count, order_size, order_size),
        lax.all_gather(root_right, "dp", axis=1, tiled=True),
    )


def per_device(
    grads,
    owner_map,
    stat_left,
    stat_right,
    root_left,
    root_right,
    master,
    moment_first,
    moment_second,
):
    owners, groups = lax.axis_size("own"), lax.axis_size("dp")
    slot_count, rows_dev, order_size = stat_left.shape
    blocks = owner_map.shape[0]
    owned_slots = owners * slot_count
    matches = owner_map[:, None] == jnp.arange(owned_slots, dtype=jnp.int32)[None, :]
    occupied = jnp.any(matches, axis=0)
    kernels = groups % 2 == 0 and (grads.shape[2] // groups) % 16 == 0 and (rows_dev // owners) % 16 == 0 and rows_dev % 64 == 0
    if kernels:
        pick = matches.astype(jnp.float32).reshape(-1)
        whole, right = exchange(pick, grads[0].astype(jnp.bfloat16), root_right, groups, owners)
        whole = whole.reshape(slot_count, order_size, order_size)
        right = right.reshape(slot_count, order_size, order_size)
    else:
        block_of = jnp.sum(jnp.where(matches, jnp.arange(blocks, dtype=jnp.int32)[:, None], 0), axis=0)
        whole, right = whole_by_collectives(grads, owner_map, root_right, occupied, block_of)
    first_row = lax.axis_index("dp") * rows_dev
    own_rows = lax.dynamic_slice_in_dim(whole, first_row, rows_dev, 1)
    own_cols = lax.dynamic_slice_in_dim(whole, first_row, rows_dev, 2)
    mixed = jnp.einsum("srk,skn->srn", root_left, whole, preferred_element_type=jnp.float32)
    direction = jnp.einsum(
        "srk,skn->srn", mixed.astype(jnp.bfloat16), right, preferred_element_type=jnp.float32
    )
    rows32 = own_rows.astype(jnp.float32)
    first_new = first_decay * moment_first + (1.0 - first_decay) * rows32
    second_new = second_decay * moment_second + (1.0 - second_decay) * rows32 * rows32
    adam_step = first_new / (jnp.sqrt(second_new) + 1e-08)
    square_sums = jnp.concatenate(
        [jnp.sum(adam_step * adam_step, axis=(1, 2)), jnp.sum(direction * direction, axis=(1, 2))]
    )
    if kernels:
        padded = jnp.pad(square_sums, (0, -2 * slot_count % 8))
        totals, delivered = finish(
            jnp.broadcast_to(padded[:, None], (padded.shape[0], 128)), direction, master, groups, owners
        )
        square_sums = totals[: 2 * slot_count, 0]
    else:
        square_sums = lax.psum(square_sums, "dp")
    graft = jnp.sqrt(square_sums[:slot_count]) / (jnp.sqrt(square_sums[slot_count:]) + 1e-06)
    master_new = master - learn_rate * graft[:, None, None] * direction
    if not kernels:
        shares = master_new.astype(jnp.bfloat16).reshape(slot_count, owners, rows_dev // owners, order_size)
        delivered = lax.all_to_all(shares, "own", split_axis=1, concat_axis=0, tiled=True)
    delivered = delivered.reshape(owned_slots, rows_dev // owners, order_size)
    left_new = stat_decay * stat_left + (1.0 - stat_decay) * jnp.einsum(
        "srk,snk->srn", own_rows, whole, preferred_element_type=jnp.float32
    )
    right_new = stat_decay * stat_right + (1.0 - stat_decay) * jnp.einsum(
        "skr,skn->srn", own_cols, whole, preferred_element_type=jnp.float32
    )
    occupied_mine = lax.dynamic_slice_in_dim(
        occupied, lax.axis_index("own") * slot_count, slot_count
    )[:, None, None]
    left_next = jnp.where(occupied_mine, left_new, stat_left)
    right_next = jnp.where(occupied_mine, right_new, stat_right)
    master_next = jnp.where(occupied_mine, master_new, master)
    first_next = jnp.where(occupied_mine, first_new, moment_first)
    second_next = jnp.where(occupied_mine, second_new, moment_second)
    weights_out = jnp.zeros((blocks,) + delivered.shape[1:], delivered.dtype)
    for s in range(owned_slots):
        weights_out = jnp.where(matches[:, s, None, None], delivered[s][None], weights_out)
    return (left_next, right_next, master_next, first_next, second_next, weights_out)


def solution(mesh):
    state = P("own", "dp", None)
    return jax.shard_map(
        per_device,
        mesh=mesh,
        in_specs=(P("dp", None, "own", None), P()) + (state,) * 7,
        out_specs=(state,) * 5 + (P(None, ("dp", "own"), None),),
        check_vma=False,
    )
```
